32 devices in a mesh: param: 2 (over x), row: 4 (over z), col: 4 (over y, core).
Axes of the slice: x: 2, y: 2, z: 4, core: 2. Of those that a mesh axis runs over, the one named last changes fastest.
Arguments:
- coefficients: bfloat16 [3, 2, 32, 512], P(None, None, 'row', 'col'), may hold values from -6 to 6
- noise_sigma: float32 [2, 32, 512], P(None, 'row', 'col'), may hold values from 0.5 to 4
- residual: float32 [2, 32, 512], P(None, 'row', 'col'), may hold values from -0.6 to 0.6
- crack_mask: int32 [32, 4], P('row', 'col'), may hold values 0 or 1
- node_panel: bfloat16 [4, 64, 3, 2048], P('row', 'col', None, 'param'), may hold values from -0.41992188 to 0.41992188
Outputs:
- hessian: float32 [2048, 2048], P('param', ('row', 'col'))
- gradient: float32 [2048], P(('param', 'row', 'col'))
The draws below stay inside these ranges and needn't reach their ends.
All inputs are finite; a program needn't handle non-finite values. No bound on the sum of `crack_mask` on one device may be relied on, other than what follows from the above.
Results may differ from the reference program's by a relative error of at most 0.0055.
Values may be sent and summed in bfloat16 or wider, within the bound.
A program may use at most 64 MiB of HBM per device.

```python
import math
import jax
import jax.numpy as jnp
from jax import lax

P_SIZE = 2048
EL = 8
CAMS = 2
NROWS = 32
NCOLS = 512
NR = 4
NC = 64


def set_ends(entries, own_key, low, largest):
    extent = entries.shape
    place = [jax.random.randint(jax.random.fold_in(own_key, axis), (), 0, extent[axis]) for axis in range(len(extent))]
    entries = entries.at[tuple(place)].set(low)
    longest = extent.index(max(extent))
    place[longest] = (place[longest] + 1) % extent[longest]
    return entries.at[tuple(place)].set(largest)


def levels(rng, shape, pieces, smallest, high):
    def one(dim, parts):
        draws = jax.random.uniform(jax.random.fold_in(jax.random.fold_in(rng, 6), dim), (parts,), jnp.float32, smallest / len(pieces), high / len(pieces))
        return jnp.repeat(jnp.exp(draws), shape[dim] // parts).reshape((-1,) + (1,) * (len(shape) - dim - 1))

    level = one(*pieces[0])
    for cut in pieces[1:]:
        level = level * one(*cut)
    return level


def noise(own_key, extent, width, limit, split=(), kind=jnp.bfloat16):
    array = width * jax.random.normal(own_key, extent, jnp.float32)
    if split:
        array = array * levels(own_key, extent, split, -0.22, 0.18)
    return jnp.clip(array, -limit, limit).astype(kind)


def setup_inputs(seed: int = 0) -> dict:
    splits = jax.random.split(jax.random.key(seed), 6)
    coefficients = noise(splits[0], (3, CAMS, NROWS, NCOLS), 1.0, 6.0, ((2, 4), (3, 4)))
    noise_sigma = jnp.clip(jnp.exp(math.log(4.0) - 2.0794415 * jax.random.uniform(splits[1], (CAMS, NROWS, NCOLS), jnp.float32) ** levels(splits[1], (CAMS, NROWS, NCOLS), ((1, 4), (2, 4)), -0.2, 0.2)), 0.5, 4.0)
    residual = noise(splits[2], (CAMS, NROWS, NCOLS), 0.1, 0.6, ((1, 4), (2, 4)), jnp.float32)
    crack_mask = set_ends((jax.random.randint(splits[3], (NROWS, NCOLS // 128), 0, 4) < 3).astype(jnp.int32), jax.random.fold_in(splits[3], 1), 0, 1)
    node_panel = noise(splits[4], (NR, NC, 3, P_SIZE), 0.07, 0.41992188, ((0, 4), (1, 4), (3, 2)))
    return dict(coefficients=coefficients, noise_sigma=noise_sigma, residual=residual, crack_mask=crack_mask, node_panel=node_panel)


def corner_shapes(rows, cols):
    vertical = ((jnp.arange(rows) % EL).astype(jnp.float32) + 0.5) / EL
    horizontal = ((jnp.arange(cols) % EL).astype(jnp.float32) + 0.5) / EL
    lower = vertical[:, None]
    right = horizontal[None, :]
    return jnp.stack([(1.0 - lower) * (1.0 - right), (1.0 - lower) * right, lower * (1.0 - right), lower * right])


def reference(coefficients, noise_sigma, residual, crack_mask, node_panel):
    extended = jnp.pad(node_panel, ((0, 1), (0, 1), (0, 0), (0, 0)))
    shapes = corner_shapes(EL, NCOLS)

    def strip(totals, index):
        hess_sum, grad_sum = totals
        first = (index * EL).astype(jnp.int32)
        coef_rows = lax.dynamic_slice_in_dim(coefficients, first, EL, 2).astype(jnp.float32)
        sigma_rows = lax.dynamic_slice_in_dim(noise_sigma, first, EL, 1)
        resid_rows = lax.dynamic_slice_in_dim(residual, first, EL, 1)
        mask_rows = lax.dynamic_slice_in_dim(crack_mask, first, EL, 0)
        live_rows = jnp.repeat(mask_rows.astype(jnp.float32), 128, axis=1)
        pixel_scale = live_rows[None] / sigma_rows
        design = ((shapes[:, None, None] * pixel_scale[None, None]) * coef_rows[None]).astype(jnp.bfloat16)
        design = design.reshape(4, 3, CAMS, EL, NC, EL).transpose(0, 1, 4, 2, 3, 5).reshape(12, NC, CAMS * EL * EL)
        nodes = lax.dynamic_slice_in_dim(extended, index.astype(jnp.int32), 2, 0)
        corners = jnp.stack([nodes[0, :-1], nodes[0, 1:], nodes[1, :-1], nodes[1, 1:]], axis=1)
        corners = corners.reshape(NC, 12, P_SIZE)
        sensitivity = jnp.einsum("kep,ekq->epq", design.astype(jnp.float32), corners.astype(jnp.float32),
                                 precision=lax.Precision.HIGHEST).astype(jnp.bfloat16)
        flat = sensitivity.reshape(NC * CAMS * EL * EL, P_SIZE)
        weighted = (pixel_scale * resid_rows).astype(jnp.bfloat16)
        weighted = weighted.reshape(CAMS, EL, NC, EL).transpose(2, 0, 1, 3).reshape(NC * CAMS * EL * EL)
        hess_sum = hess_sum + jnp.dot(flat.T, flat, preferred_element_type=jnp.float32)
        grad_sum = grad_sum + jnp.dot(weighted, flat, preferred_element_type=jnp.float32)
        return (hess_sum, grad_sum), None

    start = (jnp.zeros((P_SIZE, P_SIZE), jnp.float32), jnp.zeros((P_SIZE,), jnp.float32))
    (hessian, gradient), _ = lax.scan(strip, start, jnp.arange(NR, dtype=jnp.int32))
    return hessian, gradient
```

```python
import functools

import jax
import jax.numpy as jnp
from jax import lax
from jax.experimental import pallas as pl
from jax.experimental.pallas import tpu as pltpu
from jax.sharding import PartitionSpec as P

EL = 8
CAMS = 2
CORNERS = ((0, 0), (0, 1), (1, 0), (1, 1))
PAIRS = [(i, j) for i in range(12) for j in range(i, 12)]
PAIR_ROW = {pair: row for row, pair in enumerate(PAIRS)}
FORCE_ROW = len(PAIRS)
UP, DOWN, ACROSS, CORE, PEER = range(5)
MESH = pl.DeviceIdType.MESH


def shifted(block, axis, distance):
    devices = range(lax.axis_size(axis))
    route = [(i - distance, i) for i in devices if i - distance in devices]
    return lax.ppermute(block, axis, route)


def corner_shapes(rows, cols):
    vertical = ((jnp.arange(rows) % EL).astype(jnp.float32) + 0.5) / EL
    horizontal = ((jnp.arange(cols) % EL).astype(jnp.float32) + 0.5) / EL
    lower = vertical[:, None]
    right = horizontal[None, :]
    return jnp.stack(
        [(1.0 - lower) * (1.0 - right), (1.0 - lower) * right, lower * (1.0 - right), lower * right]
    )


def pixel_rows(design, extended):
    corners = jnp.stack(
        [extended[:-1, :-1], extended[:-1, 1:], extended[1:, :-1], extended[1:, 1:]], axis=2
    )
    width = extended.shape[3]
    corners = corners.reshape(design.shape[1], 12, width)
    sensitivity = jnp.einsum("kep,ekq->epq", design, corners, preferred_element_type=jnp.float32)
    return sensitivity.astype(jnp.bfloat16).reshape(design.shape[1] * design.shape[2], width)


def block_product(own_rows, other_rows):
    return lax.dot_general(
        own_rows, other_rows, (((0,), (0,)), ((), ())), preferred_element_type=jnp.float32
    )


def plain(coefficients, noise_sigma, residual, crack_mask, node_panel):
    rows = noise_sigma.shape[1]
    cols = noise_sigma.shape[2]
    elem_rows = rows // EL
    elem_cols = cols // EL
    shapes = corner_shapes(rows, cols)
    live_rows = jnp.repeat(crack_mask.astype(jnp.float32), 128, axis=1)
    pixel_scale = live_rows[None] / noise_sigma
    design = (
        shapes[:, None, None] * pixel_scale[None, None] * coefficients.astype(jnp.float32)[None]
    ).astype(jnp.bfloat16)
    design = design.reshape(4, 3, CAMS, elem_rows, EL, elem_cols, EL).transpose(0, 1, 3, 5, 2, 4, 6)
    design = design.reshape(12, elem_rows * elem_cols, CAMS * EL * EL)
    weighted = (pixel_scale * residual).astype(jnp.bfloat16)
    weighted = (
        weighted.reshape(CAMS, elem_rows, EL, elem_cols, EL).transpose(1, 3, 0, 2, 4).reshape(-1)
    )
    right_edge = shifted(node_panel[:, :1], "col", -1)
    widened = jnp.concatenate([node_panel, right_edge], axis=1)
    lower_edge = shifted(widened, "row", -1)
    extended = jnp.concatenate([widened, lower_edge], axis=0)
    own_rows = pixel_rows(design, extended)
    grad_part = jnp.dot(weighted, own_rows, preferred_element_type=jnp.float32)
    block = block_product(
        own_rows, pixel_rows(design, lax.all_gather(extended, "param", axis=3, tiled=True))
    )
    return (
        lax.psum_scatter(block, ("row", "col"), scatter_dimension=1, tiled=True),
        lax.psum_scatter(grad_part, ("row", "col"), scatter_dimension=0, tiled=True),
    )


def element_grams(coef_ref, sigma_ref, resid_ref, mask_ref):
    live = jnp.broadcast_to(mask_ref[...].astype(jnp.float32), (8, 128))
    y = lax.broadcasted_iota(jnp.int32, (8, 128), 0).astype(jnp.float32)
    x = (lax.broadcasted_iota(jnp.int32, (8, 128), 1) % EL).astype(jnp.float32)
    v = (y + 0.5) / EL
    u = (x + 0.5) / EL
    scale = [live / sigma_ref[c] for c in range(CAMS)]

    def rounded(value):
        return value.astype(jnp.bfloat16).astype(jnp.float32)

    coef = [[coef_ref[k, c].astype(jnp.float32) for c in range(CAMS)] for k in range(3)]
    weighted = [rounded(scale[c] * resid_ref[c]) for c in range(CAMS)]
    design = []
    for a, b in CORNERS:
        shape = (v if a else 1.0 - v) * (u if b else 1.0 - u)
        placed = [shape * scale[c] for c in range(CAMS)]
        for k in range(3):
            design.append([rounded(placed[c] * coef[k][c]) for c in range(CAMS)])

    def row(one, other):
        total = one[0] * other[0] + one[1] * other[1]
        return jnp.sum(total, axis=0, keepdims=True)

    rows = [row(design[i], design[j]) for i, j in PAIRS]
    rows += [row(design[i], weighted) for i in range(12)]
    rows.append(jnp.zeros((128 - len(rows), 128), jnp.float32))
    sums = jnp.concatenate(rows, axis=0)
    element = lax.broadcasted_iota(jnp.int32, (16, 128), 0)
    pixel = lax.broadcasted_iota(jnp.int32, (16, 128), 1)
    segment = (pixel // EL == element).astype(jnp.float32)
    return lax.dot_general(
        segment, sums, (((1,), (1,)), ((), ())),
        precision=lax.Precision.HIGHEST, preferred_element_type=jnp.float32,
    )


def assemble(grams_ref, moved_ref, stiff_ref, wide_ref, nodes, width):
    turned = grams_ref[...].T
    node = lax.broadcasted_iota(jnp.int32, (1, nodes), 1)
    node_row, node_col = node // width, node % width
    for n, (a, b) in enumerate(CORNERS):
        ok = (node_row >= a) & (node_col >= b)
        shift = a * width + b
        moved = pltpu.roll(turned, shift, 1) if shift else turned
        moved_ref[n] = jnp.where(ok, moved, 0.0)
    has_right = node_col < width - 1

    def gram_row(n, k, m, l):
        i, j = 3 * n + k, 3 * m + l
        return moved_ref[m, pl.ds(PAIR_ROW[(min(i, j), max(i, j))], 1), :]

    place = lax.broadcasted_iota(jnp.int32, (nodes, nodes), 0) - lax.broadcasted_iota(
        jnp.int32, (nodes, nodes), 1
    )
    for k in range(3):
        for l in range(3):
            bands = {}
            for n, (a, b) in enumerate(CORNERS):
                for m, (a2, b2) in enumerate(CORNERS):
                    term = gram_row(n, k, m, l)
                    if b > b2:
                        term = jnp.where(has_right, term, 0.0)
                    offset = (a - a2) * width + b - b2
                    bands[offset] = bands[offset] + term if offset in bands else term
            block = jnp.zeros((nodes, nodes), jnp.float32)
            for offset, band in bands.items():
                block = jnp.where(place == offset, band, block)
            stiff_ref[k * nodes:(k + 1) * nodes, l * nodes:(l + 1) * nodes] = block.astype(
                jnp.bfloat16
            )
    parts = []
    for k in range(3):
        force = moved_ref[0, pl.ds(FORCE_ROW + k, 1), :]
        for m in range(1, 4):
            force = force + moved_ref[m, pl.ds(FORCE_ROW + 3 * m + k, 1), :]
        parts.append(force)
    force = jnp.concatenate(parts, axis=1)
    high = force.astype(jnp.bfloat16).astype(jnp.float32)
    low = force - high
    which = lax.broadcasted_iota(jnp.int32, (16, 3 * nodes), 0)
    wide_ref[128:144, :] = jnp.where(
        which == 0, high, jnp.where(which == 1, low, 0.0)
    ).astype(jnp.bfloat16)


def kernel(
    sizes, coef_ref, sigma_ref, resid_ref, mask_ref, panel_ref, hess_ref, grad_ref,
    held, picked, grams, moved, stiff, wide, line,
    send_sem, recv_sem, gram_send, gram_recv, peer_recv,
):
    depth, columns, share = sizes
    tiles = depth * columns
    nodes = tiles * 16
    width = columns * 16
    param, z, col = lax.axis_index("param"), lax.axis_index("row"), lax.axis_index("col")
    y, c = col // 2, col % 2
    mine = z * columns + col
    per_share = share // 128
    owner = mine // per_share
    is_owner = owner == param
    first_column = pl.multiple_of((mine % per_share) * 128, 128)
    targets = {
        UP: (param, z + 1, col),
        DOWN: (param, z - 1, col),
        ACROSS: (param, z, (1 - y) * 2 + c),
        CORE: (param, z, y * 2 + 1 - c),
        PEER: (1 - param, z, col),
    }
    exists = {UP: z < depth - 1, DOWN: z > 0}

    def tile(zz, yy, cc):
        return zz * columns + yy * 2 + cc

    def rows_of(t):
        return pl.ds(pl.multiple_of(t * 16, 16), 16)

    def block_copy(t, way):
        if way == PEER:
            return pltpu.make_async_remote_copy(
                src_ref=held.at[:, rows_of(t), pl.ds(first_column, 128)],
                dst_ref=picked.at[:, rows_of(t), :],
                send_sem=send_sem.at[way, t], recv_sem=peer_recv.at[t],
                device_id=targets[way], device_id_type=MESH,
            )
        return pltpu.make_async_remote_copy(
            src_ref=held.at[:, rows_of(t), :], dst_ref=held.at[:, rows_of(t), :],
            send_sem=send_sem.at[way, t], recv_sem=recv_sem.at[t],
            device_id=targets[way], device_id_type=MESH,
        )

    def gram_copy(t, way):
        return pltpu.make_async_remote_copy(
            src_ref=grams.at[rows_of(t), :], dst_ref=grams.at[rows_of(t), :],
            send_sem=gram_send.at[way, t], recv_sem=gram_recv.at[t],
            device_id=targets[way], device_id_type=MESH,
        )

    def guarded(condition, action):
        if condition is None:
            action()
        else:
            pl.when(condition)(action)

    sent = []

    def both(one, other):
        if one is None:
            return other
        return one if other is None else one & other

    def send_block(t, ways, condition=None):
        for way in ways:
            when = both(condition, exists.get(way))
            guarded(when, lambda: block_copy(t, way).start())
            sent.append((when, block_copy, t, way))
        when = both(condition, is_owner)
        guarded(when, lambda: block_copy(t, PEER).start())
        sent.append((when, block_copy, t, PEER))

    def send_gram(t, ways, condition=None):
        for way in ways:
            when = both(condition, exists.get(way))
            guarded(when, lambda: gram_copy(t, way).start())
            sent.append((when, gram_copy, t, way))

    def pass_on(t, ways, condition=None):
        guarded(condition, lambda: block_copy(t, CORE).wait_recv())
        send_block(t, ways, condition)
        guarded(condition, lambda: gram_copy(t, CORE).wait_recv())
        send_gram(t, ways, condition)

    barrier = pltpu.get_barrier_semaphore()
    for way in range(5):
        guarded(
            exists.get(way),
            lambda: pl.semaphore_signal(
                barrier, inc=1, device_id=targets[way], device_id_type=MESH
            ),
        )
    held[:, rows_of(mine), :] = panel_ref[...]
    partners = 3 + jnp.where(z > 0, 1, 0) + jnp.where(z < depth - 1, 1, 0)
    pl.semaphore_wait(barrier, partners)

    send_block(mine, (UP, DOWN, ACROSS, CORE))
    grams[rows_of(mine), :] = element_grams(coef_ref, sigma_ref, resid_ref, mask_ref)
    send_gram(mine, (UP, DOWN, ACROSS, CORE))

    pass_on(tile(z, 1 - y, c), (CORE,))
    for k in range(1, depth):
        below, above = z - k >= 0, z + k < depth
        pass_on(tile(z - k, y, c), (UP, ACROSS, CORE), below)
        pass_on(tile(z + k, y, c), (DOWN, ACROSS, CORE), above)
        if k > 1:
            pass_on(tile(z - k + 1, 1 - y, c), (CORE,), z - k + 1 >= 0)
            pass_on(tile(z + k - 1, 1 - y, c), (CORE,), z + k - 1 < depth)
    k = depth
    pass_on(tile(z - k + 1, 1 - y, c), (CORE,), z - k + 1 >= 0)
    pass_on(tile(z + k - 1, 1 - y, c), (CORE,), z + k - 1 < depth)
    for zz in range(depth):
        for yy in range(2):
            pass_on(tile(zz, yy, 1 - c), ())

    assemble(grams, moved, stiff, wide, nodes, width)

    @pl.when(is_owner)
    def _():
        picked[...] = held[:, :, pl.ds(first_column, 128)]

    @pl.when(jnp.logical_not(is_owner))
    def _():
        for t in range(tiles):
            block_copy(t, PEER).wait_recv()

    chosen = picked[...].reshape(3 * nodes, 128)
    turned = lax.dot_general(
        chosen, stiff[...], (((0,), (0,)), ((), ())), preferred_element_type=jnp.float32
    )
    wide[0:128, :] = turned.astype(jnp.bfloat16)
    product = jnp.dot(
        wide[...], held[...].reshape(3 * nodes, share), preferred_element_type=jnp.float32
    )
    hess_ref[...] = product[:128].T
    line[...] = jnp.broadcast_to(product[128:129] + product[129:130], (8, share))
    pair = line[0:1, pl.ds(pl.multiple_of((mine // 2) * 128, 128), 128)]
    pair = jnp.where(mine % 2 == 1, pltpu.roll(pair, 64, 1), pair)
    grad_ref[...] = pair[:, :64]

    for when, copy, t, way in sent:
        guarded(when, lambda: copy(t, way).wait_send())


def gathered(sizes, coefficients, noise_sigma, residual, crack_mask, node_panel):
    depth, columns, share = sizes
    tiles = depth * columns
    nodes = tiles * 16
    panel = node_panel[0].transpose(1, 0, 2)
    hessian, gradient = pl.pallas_call(
        functools.partial(kernel, sizes),
        out_shape=(
            jax.ShapeDtypeStruct((share, 128), jnp.float32),
            jax.ShapeDtypeStruct((1, 64), jnp.float32),
        ),
        in_specs=[pl.BlockSpec(memory_space=pltpu.VMEM)] * 5,
        out_specs=[pl.BlockSpec(memory_space=pltpu.VMEM)] * 2,
        scratch_shapes=[
            pltpu.VMEM((3, nodes, share), jnp.bfloat16),
            pltpu.VMEM((3, nodes, 128), jnp.bfloat16),
            pltpu.VMEM((nodes, 128), jnp.float32),
            pltpu.VMEM((4, 128, nodes), jnp.float32),
            pltpu.VMEM((3 * nodes, 3 * nodes), jnp.bfloat16),
            pltpu.VMEM((144, 3 * nodes), jnp.bfloat16),
            pltpu.VMEM((8, share), jnp.float32),
            pltpu.SemaphoreType.DMA((5, tiles)),
            pltpu.SemaphoreType.DMA((tiles,)),
            pltpu.SemaphoreType.DMA((4, tiles)),
            pltpu.SemaphoreType.DMA((tiles,)),
            pltpu.SemaphoreType.DMA((tiles,)),
        ],
        compiler_params=pltpu.CompilerParams(
            collective_id=0, has_side_effects=True, vmem_limit_bytes=32 * 2**20
        ),
    )(coefficients, noise_sigma, residual, crack_mask, panel)
    return hessian, gradient.reshape(64)


def solution(mesh):
    def on_device(coefficients, noise_sigma, residual, crack_mask, node_panel):
        depth, columns, share = mesh.shape["row"], mesh.shape["col"], node_panel.shape[3]
        fits = (
            mesh.shape["param"] == 2
            and columns == 4
            and noise_sigma.shape == (CAMS, EL, 128)
            and node_panel.shape[:3] == (1, 16, 3)
            and share == 64 * depth * columns
        )
        if fits:
            return gathered(
                (depth, columns, share), coefficients, noise_sigma, residual, crack_mask, node_panel
            )
        return plain(coefficients, noise_sigma, residual, crack_mask, node_panel)

    in_specs = (
        P(None, None, "row", "col"),
        P(None, "row", "col"),
        P(None, "row", "col"),
        P("row", "col"),
        P("row", "col", None, "param"),
    )
    out_specs = (P("param", ("row", "col")), P(("param", "row", "col")))
    return jax.shard_map(
        on_device, mesh=mesh, in_specs=in_specs, out_specs=out_specs, check_vma=False
    )
```

```python
import functools

import jax
import jax.numpy as jnp
from jax import lax
from jax.experimental import pallas as pl
from jax.experimental.pallas import tpu as pltpu
from jax.sharding import PartitionSpec as P

EL = 8
CAMS = 2
CORNERS = ((0, 0), (0, 1), (1, 0), (1, 1))
PAIRS = [(i, j) for i in range(12) for j in range(i, 12)]
PAIR_ROW = {pair: row for row, pair in enumerate(PAIRS)}
FORCE_ROW = len(PAIRS)
UP, DOWN, ACROSS, CORE, PEER = range(5)
MESH = pl.DeviceIdType.MESH


def shifted(block, axis, distance):
    devices = range(lax.axis_size(axis))
    route = [(i - distance, i) for i in devices if i - distance in devices]
    return lax.ppermute(block, axis, route)


def corner_shapes(rows, cols):
    vertical = ((jnp.arange(rows) % EL).astype(jnp.float32) + 0.5) / EL
    horizontal = ((jnp.arange(cols) % EL).astype(jnp.float32) + 0.5) / EL
    lower = vertical[:, None]
    right = horizontal[None, :]
    return jnp.stack(
        [(1.0 - lower) * (1.0 - right), (1.0 - lower) * right, lower * (1.0 - right), lower * right]
    )


def pixel_rows(design, extended):
    corners = jnp.stack(
        [extended[:-1, :-1], extended[:-1, 1:], extended[1:, :-1], extended[1:, 1:]], axis=2
    )
    width = extended.shape[3]
    corners = corners.reshape(design.shape[1], 12, width)
    sensitivity = jnp.einsum("kep,ekq->epq", design, corners, preferred_element_type=jnp.float32)
    return sensitivity.astype(jnp.bfloat16).reshape(design.shape[1] * design.shape[2], width)


def block_product(own_rows, other_rows):
    return lax.dot_general(
        own_rows, other_rows, (((0,), (0,)), ((), ())), preferred_element_type=jnp.float32
    )


def plain(coefficients, noise_sigma, residual, crack_mask, node_panel):
    rows = noise_sigma.shape[1]
    cols = noise_sigma.shape[2]
    elem_rows = rows // EL
    elem_cols = cols // EL
    shapes = corner_shapes(rows, cols)
    live_rows = jnp.repeat(crack_mask.astype(jnp.float32), 128, axis=1)
    pixel_scale = live_rows[None] / noise_sigma
    design = (
        shapes[:, None, None] * pixel_scale[None, None] * coefficients.astype(jnp.float32)[None]
    ).astype(jnp.bfloat16)
    design = design.reshape(4, 3, CAMS, elem_rows, EL, elem_cols, EL).transpose(0, 1, 3, 5, 2, 4, 6)
    design = design.reshape(12, elem_rows * elem_cols, CAMS * EL * EL)
    weighted = (pixel_scale * residual).astype(jnp.bfloat16)
    weighted = (
        weighted.reshape(CAMS, elem_rows, EL, elem_cols, EL).transpose(1, 3, 0, 2, 4).reshape(-1)
    )
    right_edge = shifted(node_panel[:, :1], "col", -1)
    widened = jnp.concatenate([node_panel, right_edge], axis=1)
    lower_edge = shifted(widened, "row", -1)
    extended = jnp.concatenate([widened, lower_edge], axis=0)
    own_rows = pixel_rows(design, extended)
    grad_part = jnp.dot(weighted, own_rows, preferred_element_type=jnp.float32)
    block = block_product(
        own_rows, pixel_rows(design, lax.all_gather(extended, "param", axis=3, tiled=True))
    )
    return (
        lax.psum_scatter(block, ("row", "col"), scatter_dimension=1, tiled=True),
        lax.psum_scatter(grad_part, ("row", "col"), scatter_dimension=0, tiled=True),
    )


def element_grams(coef_ref, sigma_ref, resid_ref, mask_ref):
    mask = jnp.broadcast_to(mask_ref[...].astype(jnp.float32), (8, 8))
    own = lax.broadcasted_iota(jnp.int32, (8, 8), 0) == lax.broadcasted_iota(jnp.int32, (8, 8), 1)
    live = jnp.sum(jnp.where(own, mask, 0.0), axis=1, keepdims=True)
    live = jnp.broadcast_to(live, (8, 128))
    y = lax.broadcasted_iota(jnp.int32, (8, 128), 0).astype(jnp.float32)
    x = (lax.broadcasted_iota(jnp.int32, (8, 128), 1) % EL).astype(jnp.float32)
    v = (y + 0.5) / EL
    u = (x + 0.5) / EL
    scale = [live / sigma_ref[c] for c in range(CAMS)]

    def rounded(value):
        return value.astype(jnp.bfloat16).astype(jnp.float32)

    coef = [[coef_ref[k, c].astype(jnp.float32) for c in range(CAMS)] for k in range(3)]
    weighted = [rounded(scale[c] * resid_ref[c]) for c in range(CAMS)]
    design = []
    for a, b in CORNERS:
        shape = (v if a else 1.0 - v) * (u if b else 1.0 - u)
        placed = [shape * scale[c] for c in range(CAMS)]
        for k in range(3):
            design.append([rounded(placed[c] * coef[k][c]) for c in range(CAMS)])

    def row(one, other):
        total = one[0] * other[0] + one[1] * other[1]
        return jnp.sum(total, axis=0, keepdims=True)

    rows = [row(design[i], design[j]) for i, j in PAIRS]
    rows += [row(design[i], weighted) for i in range(12)]
    rows.append(jnp.zeros((128 - len(rows), 128), jnp.float32))
    sums = jnp.concatenate(rows, axis=0)
    element = lax.broadcasted_iota(jnp.int32, (16, 128), 0)
    pixel = lax.broadcasted_iota(jnp.int32, (16, 128), 1)
    segment = (pixel // EL == element).astype(jnp.float32)
    return lax.dot_general(
        segment, sums, (((1,), (1,)), ((), ())),
        precision=lax.Precision.HIGHEST, preferred_element_type=jnp.float32,
    )


def corner_moves(grams_ref, moved_ref, wide_ref, nodes, width):
    turned = grams_ref[...].T
    node = lax.broadcasted_iota(jnp.int32, (1, nodes), 1)
    node_row, node_col = node // width, node % width
    for n, (a, b) in enumerate(CORNERS):
        ok = (node_row >= a) & (node_col >= b)
        shift = a * width + b
        moved = pltpu.roll(turned, shift, 1) if shift else turned
        moved_ref[n] = jnp.where(ok, moved, 0.0)
    parts = []
    for k in range(3):
        force = moved_ref[0, pl.ds(FORCE_ROW + k, 1), :]
        for m in range(1, 4):
            force = force + moved_ref[m, pl.ds(FORCE_ROW + 3 * m + k, 1), :]
        parts.append(force)
    force = jnp.concatenate(parts, axis=1)
    high = force.astype(jnp.bfloat16).astype(jnp.float32)
    low = force - high
    which = lax.broadcasted_iota(jnp.int32, (16, 3 * nodes), 0)
    wide_ref[128:144, :] = jnp.where(
        which == 0, high, jnp.where(which == 1, low, 0.0)
    ).astype(jnp.bfloat16)


def assemble(moved_ref, stiff_ref, nodes, width, blocks):
    node_col = lax.broadcasted_iota(jnp.int32, (1, nodes), 1) % width
    has_right = node_col < width - 1

    def gram_row(n, k, m, l):
        i, j = 3 * n + k, 3 * m + l
        return moved_ref[m, pl.ds(PAIR_ROW[(min(i, j), max(i, j))], 1), :]

    place = lax.broadcasted_iota(jnp.int32, (nodes, nodes), 0) - lax.broadcasted_iota(
        jnp.int32, (nodes, nodes), 1
    )
    for k, l in blocks:
        bands = {}
        for n, (a, b) in enumerate(CORNERS):
            for m, (a2, b2) in enumerate(CORNERS):
                term = gram_row(n, k, m, l)
                if b > b2:
                    term = jnp.where(has_right, term, 0.0)
                offset = (a - a2) * width + b - b2
                bands[offset] = bands[offset] + term if offset in bands else term
        block = jnp.zeros((nodes, nodes), jnp.float32)
        for offset, band in bands.items():
            block = jnp.where(place == offset, band, block)
        stiff_ref[k * nodes:(k + 1) * nodes, l * nodes:(l + 1) * nodes] = block.astype(
            jnp.bfloat16
        )


def kernel(
    sizes, coef_hbm, sigma_hbm, resid_hbm, mask_hbm, panel_hbm, hess_ref, grad_ref,
    coef_ref, sigma_ref, resid_ref, mask_ref, held, picked, grams, moved, stiff, wide, line,
    load_sem, send_sem, recv_sem, gram_send, gram_recv, peer_recv,
):
    depth, columns, share = sizes
    tiles = depth * columns
    nodes = tiles * 16
    width = columns * 16
    param, z, col = lax.axis_index("param"), lax.axis_index("row"), lax.axis_index("col")
    y, c = col // 2, col % 2
    mine = z * columns + col
    per_share = share // 128
    owner = mine // per_share
    is_owner = owner == param
    first_column = pl.multiple_of((mine % per_share) * 128, 128)
    targets = {
        UP: (param, z + 1, col),
        DOWN: (param, z - 1, col),
        ACROSS: (param, z, (1 - y) * 2 + c),
        CORE: (param, z, y * 2 + 1 - c),
        PEER: (1 - param, z, col),
    }
    exists = {UP: z < depth - 1, DOWN: z > 0}

    def tile(zz, yy, cc):
        return zz * columns + yy * 2 + cc

    def rows_of(t):
        return pl.ds(pl.multiple_of(t * 16, 16), 16)

    def block_copy(t, way):
        if way == PEER:
            return pltpu.make_async_remote_copy(
                src_ref=held.at[:, rows_of(t), pl.ds(first_column, 128)],
                dst_ref=picked.at[:, rows_of(t), :],
                send_sem=send_sem.at[way, t], recv_sem=peer_recv.at[t],
                device_id=targets[way], device_id_type=MESH,
            )
        return pltpu.make_async_remote_copy(
            src_ref=held.at[:, rows_of(t), :], dst_ref=held.at[:, rows_of(t), :],
            send_sem=send_sem.at[way, t], recv_sem=recv_sem.at[t],
            device_id=targets[way], device_id_type=MESH,
        )

    def peer_of(step):
        other = lax.rem(mine + step, tiles)
        return other, (param, other // columns, other % columns)

    def gram_copy(t, step):
        return pltpu.make_async_remote_copy(
            src_ref=grams.at[rows_of(t), :], dst_ref=grams.at[rows_of(t), :],
            send_sem=gram_send.at[step], recv_sem=gram_recv.at[t],
            device_id=peer_of(step)[1], device_id_type=MESH,
        )

    def guarded(condition, action):
        if condition is None:
            action()
        else:
            pl.when(condition)(action)

    sent = []

    def both(one, other):
        if one is None:
            return other
        return one if other is None else one & other

    def send_block(t, ways, condition=None):
        for way in ways:
            when = both(condition, exists.get(way))
            guarded(when, lambda: block_copy(t, way).start())
            sent.append((when, block_copy, t, way))
        when = both(condition, is_owner)
        guarded(when, lambda: block_copy(t, PEER).start())
        sent.append((when, block_copy, t, PEER))

    def pass_on(t, ways, condition=None):
        guarded(condition, lambda: block_copy(t, CORE).wait_recv())
        send_block(t, ways, condition)

    loads = [
        pltpu.make_async_copy(panel_hbm, held.at[:, rows_of(mine), :], load_sem.at[0]),
        pltpu.make_async_copy(mask_hbm, mask_ref, load_sem.at[1]),
        pltpu.make_async_copy(sigma_hbm, sigma_ref, load_sem.at[2]),
        pltpu.make_async_copy(coef_hbm, coef_ref, load_sem.at[3]),
        pltpu.make_async_copy(resid_hbm, resid_ref, load_sem.at[4]),
    ]
    for load in loads:
        load.start()
    barrier = pltpu.get_barrier_semaphore()
    pl.semaphore_signal(barrier, inc=1, device_id=targets[PEER], device_id_type=MESH)
    for step in range(1, tiles):
        pl.semaphore_signal(barrier, inc=1, device_id=peer_of(step)[1], device_id_type=MESH)
    loads[0].wait()
    pl.semaphore_wait(barrier, tiles)

    send_block(mine, (UP, DOWN, ACROSS, CORE))
    for load in loads[1:]:
        load.wait()
    grams[rows_of(mine), :] = element_grams(coef_ref, sigma_ref, resid_ref, mask_ref)
    for step in range(1, tiles):
        gram_copy(mine, step).start()

    pairs = [(k, l) for k in range(3) for l in range(3)]
    pass_on(tile(z, 1 - y, c), (CORE,))
    for k in range(1, depth):
        below, above = z - k >= 0, z + k < depth
        pass_on(tile(z - k, y, c), (UP, ACROSS, CORE), below)
        pass_on(tile(z + k, y, c), (DOWN, ACROSS, CORE), above)
        if k > 1:
            pass_on(tile(z - k + 1, 1 - y, c), (CORE,), z - k + 1 >= 0)
            pass_on(tile(z + k - 1, 1 - y, c), (CORE,), z + k - 1 < depth)
        if k == 2:
            for step in range(1, tiles):
                gram_copy(peer_of(step)[0], step).wait_recv()
            corner_moves(grams, moved, wide, nodes, width)
            assemble(moved, stiff, nodes, width, pairs[:4])
    assemble(moved, stiff, nodes, width, pairs[4:])
    k = depth
    pass_on(tile(z - k + 1, 1 - y, c), (CORE,), z - k + 1 >= 0)
    pass_on(tile(z + k - 1, 1 - y, c), (CORE,), z + k - 1 < depth)
    for zz in range(depth):
        for yy in range(2):
            pass_on(tile(zz, yy, 1 - c), ())

    @pl.when(is_owner)
    def _():
        picked[...] = held[:, :, pl.ds(first_column, 128)]

    @pl.when(jnp.logical_not(is_owner))
    def _():
        for t in range(tiles):
            block_copy(t, PEER).wait_recv()

    chosen = picked[...].reshape(3 * nodes, 128)
    turned = lax.dot_general(
        chosen, stiff[...], (((0,), (0,)), ((), ())), preferred_element_type=jnp.float32
    )
    wide[0:128, :] = turned.astype(jnp.bfloat16)
    product = jnp.dot(
        wide[...], held[...].reshape(3 * nodes, share), preferred_element_type=jnp.float32
    )
    hess_ref[...] = product[:128].T
    line[...] = jnp.broadcast_to(product[128:129] + product[129:130], (8, share))
    pair = line[0:1, pl.ds(pl.multiple_of((mine // 2) * 128, 128), 128)]
    pair = jnp.where(mine % 2 == 1, pltpu.roll(pair, 64, 1), pair)
    grad_ref[...] = pair[:, :64]

    for when, copy, t, way in sent:
        guarded(when, lambda: copy(t, way).wait_send())
    for step in range(1, tiles):
        gram_copy(mine, step).wait_send()


def hand_over(hess_ref, grad_ref, hess_out, grad_out, sem):
    copies = (
        pltpu.make_async_copy(hess_ref, hess_out, sem.at[0]),
        pltpu.make_async_copy(grad_ref, grad_out, sem.at[1]),
    )
    for copy in copies:
        copy.start()
    for copy in copies:
        copy.wait()


def gathered(sizes, coefficients, noise_sigma, residual, crack_mask, node_panel):
    depth, columns, share = sizes
    tiles = depth * columns
    nodes = tiles * 16
    panel = node_panel[0].transpose(1, 0, 2)
    hessian, gradient = pl.pallas_call(
        functools.partial(kernel, sizes),
        out_shape=(
            jax.ShapeDtypeStruct((share, 128), jnp.float32),
            jax.ShapeDtypeStruct((1, 64), jnp.float32),
        ),
        in_specs=[pl.BlockSpec(memory_space=pltpu.HBM)] * 5,
        out_specs=[pl.BlockSpec(memory_space=pltpu.VMEM)] * 2,
        scratch_shapes=[
            pltpu.VMEM(coefficients.shape, jnp.bfloat16),
            pltpu.VMEM(noise_sigma.shape, jnp.float32),
            pltpu.VMEM(residual.shape, jnp.float32),
            pltpu.VMEM((1, EL), jnp.int32),
            pltpu.VMEM((3, nodes, share), jnp.bfloat16),
            pltpu.VMEM((3, nodes, 128), jnp.bfloat16),
            pltpu.VMEM((nodes, 128), jnp.float32),
            pltpu.VMEM((4, 128, nodes), jnp.float32),
            pltpu.VMEM((3 * nodes, 3 * nodes), jnp.bfloat16),
            pltpu.VMEM((144, 3 * nodes), jnp.bfloat16),
            pltpu.VMEM((8, share), jnp.float32),
            pltpu.SemaphoreType.DMA((5,)),
            pltpu.SemaphoreType.DMA((5, tiles)),
            pltpu.SemaphoreType.DMA((tiles,)),
            pltpu.SemaphoreType.DMA((tiles,)),
            pltpu.SemaphoreType.DMA((tiles,)),
            pltpu.SemaphoreType.DMA((tiles,)),
        ],
        compiler_params=pltpu.CompilerParams(
            collective_id=0, has_side_effects=True, vmem_limit_bytes=60 * 2**20
        ),
    )(coefficients, noise_sigma, residual, crack_mask.reshape(1, EL), panel)
    hessian, gradient = pl.pallas_call(
        hand_over,
        out_shape=(
            jax.ShapeDtypeStruct((share, 128), jnp.float32),
            jax.ShapeDtypeStruct((1, 64), jnp.float32),
        ),
        in_specs=[pl.BlockSpec(memory_space=pltpu.HBM)] * 2,
        out_specs=[pl.BlockSpec(memory_space=pltpu.HBM)] * 2,
        scratch_shapes=[pltpu.SemaphoreType.DMA((2,))],
        compiler_params=pltpu.CompilerParams(vmem_limit_bytes=60 * 2**20),
    )(hessian, gradient)
    return hessian, gradient.reshape(64)


def solution(mesh):
    def on_device(coefficients, noise_sigma, residual, crack_mask, node_panel):
        depth, columns, share = mesh.shape["row"], mesh.shape["col"], node_panel.shape[3]
        fits = (
            mesh.shape["param"] == 2
            and columns == 4
            and depth >= 3
            and noise_sigma.shape == (CAMS, EL, 128)
            and node_panel.shape[:3] == (1, 16, 3)
            and share == 64 * depth * columns
        )
        if fits:
            return gathered(
                (depth, columns, share), coefficients, noise_sigma, residual, crack_mask, node_panel
            )
        return plain(coefficients, noise_sigma, residual, crack_mask, node_panel)

    in_specs = (
        P(None, None, "row", "col"),
        P(None, "row", "col"),
        P(None, "row", "col"),
        P("row", "col"),
        P("row", "col", None, "param"),
    )
    out_specs = (P("param", ("row", "col")), P(("param", "row", "col")))
    return jax.shard_map(
        on_device, mesh=mesh, in_specs=in_specs, out_specs=out_specs, check_vma=False
    )
```

```python
import functools

import jax
import jax.numpy as jnp
from jax import lax
from jax.experimental import pallas as pl
from jax.experimental.pallas import tpu as pltpu
from jax.sharding import PartitionSpec as P

EL = 8
CAMS = 2
CORNERS = ((0, 0), (0, 1), (1, 0), (1, 1))
PAIRS = [(i, j) for i in range(12) for j in range(i, 12)]
PAIR_ROW = {pair: row for row, pair in enumerate(PAIRS)}
FORCE_ROW = len(PAIRS)
UP, DOWN, ACROSS, CORE, PEER = range(5)
MESH = pl.DeviceIdType.MESH


def shifted(block, axis, distance):
    devices = range(lax.axis_size(axis))
    route = [(i - distance, i) for i in devices if i - distance in devices]
    return lax.ppermute(block, axis, route)


def corner_shapes(rows, cols):
    vertical = ((jnp.arange(rows) % EL).astype(jnp.float32) + 0.5) / EL
    horizontal = ((jnp.arange(cols) % EL).astype(jnp.float32) + 0.5) / EL
    lower = vertical[:, None]
    right = horizontal[None, :]
    return jnp.stack(
        [(1.0 - lower) * (1.0 - right), (1.0 - lower) * right, lower * (1.0 - right), lower * right]
    )


def pixel_rows(design, extended):
    corners = jnp.stack(
        [extended[:-1, :-1], extended[:-1, 1:], extended[1:, :-1], extended[1:, 1:]], axis=2
    )
    width = extended.shape[3]
    corners = corners.reshape(design.shape[1], 12, width)
    sensitivity = jnp.einsum("kep,ekq->epq", design, corners, preferred_element_type=jnp.float32)
    return sensitivity.astype(jnp.bfloat16).reshape(design.shape[1] * design.shape[2], width)


def block_product(own_rows, other_rows):
    return lax.dot_general(
        own_rows, other_rows, (((0,), (0,)), ((), ())), preferred_element_type=jnp.float32
    )


def plain(coefficients, noise_sigma, residual, crack_mask, node_panel):
    rows = noise_sigma.shape[1]
    cols = noise_sigma.shape[2]
    elem_rows = rows // EL
    elem_cols = cols // EL
    shapes = corner_shapes(rows, cols)
    live_rows = jnp.repeat(crack_mask.astype(jnp.float32), 128, axis=1)
    pixel_scale = live_rows[None] / noise_sigma
    design = (
        shapes[:, None, None] * pixel_scale[None, None] * coefficients.astype(jnp.float32)[None]
    ).astype(jnp.bfloat16)
    design = design.reshape(4, 3, CAMS, elem_rows, EL, elem_cols, EL).transpose(0, 1, 3, 5, 2, 4, 6)
    design = design.reshape(12, elem_rows * elem_cols, CAMS * EL * EL)
    weighted = (pixel_scale * residual).astype(jnp.bfloat16)
    weighted = (
        weighted.reshape(CAMS, elem_rows, EL, elem_cols, EL).transpose(1, 3, 0, 2, 4).reshape(-1)
    )
    right_edge = shifted(node_panel[:, :1], "col", -1)
    widened = jnp.concatenate([node_panel, right_edge], axis=1)
    lower_edge = shifted(widened, "row", -1)
    extended = jnp.concatenate([widened, lower_edge], axis=0)
    own_rows = pixel_rows(design, extended)
    grad_part = jnp.dot(weighted, own_rows, preferred_element_type=jnp.float32)
    block = block_product(
        own_rows, pixel_rows(design, lax.all_gather(extended, "param", axis=3, tiled=True))
    )
    return (
        lax.psum_scatter(block, ("row", "col"), scatter_dimension=1, tiled=True),
        lax.psum_scatter(grad_part, ("row", "col"), scatter_dimension=0, tiled=True),
    )


def element_grams(coef_ref, sigma_ref, resid_ref, mask_ref):
    mask = jnp.broadcast_to(mask_ref[...].astype(jnp.float32), (8, 8))
    own = lax.broadcasted_iota(jnp.int32, (8, 8), 0) == lax.broadcasted_iota(jnp.int32, (8, 8), 1)
    live = jnp.sum(jnp.where(own, mask, 0.0), axis=1, keepdims=True)
    live = jnp.broadcast_to(live, (8, 128))
    y = lax.broadcasted_iota(jnp.int32, (8, 128), 0).astype(jnp.float32)
    x = (lax.broadcasted_iota(jnp.int32, (8, 128), 1) % EL).astype(jnp.float32)
    v = (y + 0.5) / EL
    u = (x + 0.5) / EL
    scale = [live / sigma_ref[c] for c in range(CAMS)]

    def rounded(value):
        return value.astype(jnp.bfloat16).astype(jnp.float32)

    coef = [[coef_ref[k, c].astype(jnp.float32) for c in range(CAMS)] for k in range(3)]
    weighted = [rounded(scale[c] * resid_ref[c]) for c in range(CAMS)]
    design = []
    for a, b in CORNERS:
        shape = (v if a else 1.0 - v) * (u if b else 1.0 - u)
        placed = [shape * scale[c] for c in range(CAMS)]
        for k in range(3):
            design.append([rounded(placed[c] * coef[k][c]) for c in range(CAMS)])

    def row(one, other):
        total = one[0] * other[0] + one[1] * other[1]
        return jnp.sum(total, axis=0, keepdims=True)

    rows = [row(design[i], design[j]) for i, j in PAIRS]
    rows += [row(design[i], weighted) for i in range(12)]
    rows.append(jnp.zeros((128 - len(rows), 128), jnp.float32))
    sums = jnp.concatenate(rows, axis=0)
    element = lax.broadcasted_iota(jnp.int32, (16, 128), 0)
    pixel = lax.broadcasted_iota(jnp.int32, (16, 128), 1)
    segment = (pixel // EL == element).astype(jnp.float32)
    return lax.dot_general(
        segment, sums, (((1,), (1,)), ((), ())),
        precision=lax.Precision.HIGHEST, preferred_element_type=jnp.float32,
    )


def corner_moves(grams_ref, moved_ref, wide_ref, nodes, width):
    turned = grams_ref[...].T
    node = lax.broadcasted_iota(jnp.int32, (1, nodes), 1)
    node_row, node_col = node // width, node % width
    for n, (a, b) in enumerate(CORNERS):
        ok = (node_row >= a) & (node_col >= b)
        shift = a * width + b
        moved = pltpu.roll(turned, shift, 1) if shift else turned
        moved_ref[n] = jnp.where(ok, moved, 0.0)
    parts = []
    for k in range(3):
        force = moved_ref[0, pl.ds(FORCE_ROW + k, 1), :]
        for m in range(1, 4):
            force = force + moved_ref[m, pl.ds(FORCE_ROW + 3 * m + k, 1), :]
        parts.append(force)
    force = jnp.concatenate(parts, axis=1)
    high = force.astype(jnp.bfloat16).astype(jnp.float32)
    low = force - high
    which = lax.broadcasted_iota(jnp.int32, (16, 3 * nodes), 0)
    wide_ref[128:144, :] = jnp.where(
        which == 0, high, jnp.where(which == 1, low, 0.0)
    ).astype(jnp.bfloat16)


def assemble(moved_ref, stiff_ref, nodes, width, blocks):
    node_col = lax.broadcasted_iota(jnp.int32, (1, nodes), 1) % width
    has_right = node_col < width - 1

    def gram_row(n, k, m, l):
        i, j = 3 * n + k, 3 * m + l
        return moved_ref[m, pl.ds(PAIR_ROW[(min(i, j), max(i, j))], 1), :]

    place = lax.broadcasted_iota(jnp.int32, (nodes, nodes), 0) - lax.broadcasted_iota(
        jnp.int32, (nodes, nodes), 1
    )
    for k, l in blocks:
        bands = {}
        for n, (a, b) in enumerate(CORNERS):
            for m, (a2, b2) in enumerate(CORNERS):
                term = gram_row(n, k, m, l)
                if b > b2:
                    term = jnp.where(has_right, term, 0.0)
                offset = (a - a2) * width + b - b2
                bands[offset] = bands[offset] + term if offset in bands else term
        block = jnp.zeros((nodes, nodes), jnp.float32)
        for offset, band in bands.items():
            block = jnp.where(place == offset, band, block)
        stiff_ref[k * nodes:(k + 1) * nodes, l * nodes:(l + 1) * nodes] = block.astype(
            jnp.bfloat16
        )


def kernel(
    sizes, coef_hbm, sigma_hbm, resid_hbm, mask_hbm, panel_hbm, hess_ref, grad_ref,
    coef_ref, sigma_ref, resid_ref, mask_ref, held, picked, grams, moved, stiff, wide, line,
    load_sem, send_sem, recv_sem, gram_send, gram_recv, peer_recv,
):
    depth, columns, share = sizes
    tiles = depth * columns
    nodes = tiles * 16
    width = columns * 16
    param, z, col = lax.axis_index("param"), lax.axis_index("row"), lax.axis_index("col")
    y, c = col // 2, col % 2
    mine = z * columns + col
    per_share = share // 128
    owner = mine // per_share
    is_owner = owner == param
    first_column = pl.multiple_of((mine % per_share) * 128, 128)
    targets = {
        UP: (param, z + 1, col),
        DOWN: (param, z - 1, col),
        ACROSS: (param, z, (1 - y) * 2 + c),
        CORE: (param, z, y * 2 + 1 - c),
        PEER: (1 - param, z, col),
    }
    exists = {UP: z < depth - 1, DOWN: z > 0}

    def tile(zz, yy, cc):
        return zz * columns + yy * 2 + cc

    def rows_of(t):
        return pl.ds(pl.multiple_of(t * 16, 16), 16)

    def block_copy(t, way):
        if way == PEER:
            return pltpu.make_async_remote_copy(
                src_ref=held.at[:, rows_of(t), pl.ds(first_column, 128)],
                dst_ref=picked.at[:, rows_of(t), :],
                send_sem=send_sem.at[way, t], recv_sem=peer_recv.at[t],
                device_id=targets[way], device_id_type=MESH,
            )
        return pltpu.make_async_remote_copy(
            src_ref=held.at[:, rows_of(t), :], dst_ref=held.at[:, rows_of(t), :],
            send_sem=send_sem.at[way, t], recv_sem=recv_sem.at[t],
            device_id=targets[way], device_id_type=MESH,
        )

    def peer_of(step):
        other = lax.rem(mine + step, tiles)
        return other, (param, other // columns, other % columns)

    def gram_copy(t, step):
        return pltpu.make_async_remote_copy(
            src_ref=grams.at[rows_of(t), :], dst_ref=grams.at[rows_of(t), :],
            send_sem=gram_send.at[step], recv_sem=gram_recv.at[t],
            device_id=peer_of(step)[1], device_id_type=MESH,
        )

    def guarded(condition, action):
        if condition is None:
            action()
        else:
            pl.when(condition)(action)

    sent = []

    def both(one, other):
        if one is None:
            return other
        return one if other is None else one & other

    def send_block(t, ways, condition=None):
        for way in ways:
            when = both(condition, exists.get(way))
            guarded(when, lambda: block_copy(t, way).start())
            sent.append((when, block_copy, t, way))
        when = both(condition, is_owner)
        guarded(when, lambda: block_copy(t, PEER).start())
        sent.append((when, block_copy, t, PEER))

    def pass_on(t, ways, condition=None):
        guarded(condition, lambda: block_copy(t, CORE).wait_recv())
        send_block(t, ways, condition)

    loads = [
        pltpu.make_async_copy(panel_hbm, held.at[:, rows_of(mine), :], load_sem.at[0]),
        pltpu.make_async_copy(mask_hbm, mask_ref, load_sem.at[1]),
        pltpu.make_async_copy(sigma_hbm, sigma_ref, load_sem.at[2]),
        pltpu.make_async_copy(coef_hbm, coef_ref, load_sem.at[3]),
        pltpu.make_async_copy(resid_hbm, resid_ref, load_sem.at[4]),
    ]
    for load in loads:
        load.start()
    barrier = pltpu.get_barrier_semaphore()
    pl.semaphore_signal(barrier, inc=1, device_id=targets[PEER], device_id_type=MESH)
    for step in range(1, tiles):
        pl.semaphore_signal(barrier, inc=1, device_id=peer_of(step)[1], device_id_type=MESH)
    loads[0].wait()
    pl.semaphore_wait(barrier, tiles)

    send_block(mine, (UP, DOWN, ACROSS, CORE))
    for load in loads[1:]:
        load.wait()
    grams[rows_of(mine), :] = element_grams(coef_ref, sigma_ref, resid_ref, mask_ref)
    for step in range(1, tiles):
        gram_copy(mine, step).start()

    pairs = [(k, l) for k in range(3) for l in range(3)]
    pass_on(tile(z, 1 - y, c), (CORE,))
    for k in range(1, depth):
        below, above = z - k >= 0, z + k < depth
        pass_on(tile(z - k, y, c), (UP, ACROSS, CORE), below)
        pass_on(tile(z + k, y, c), (DOWN, ACROSS, CORE), above)
        if k > 1:
            pass_on(tile(z - k + 1, 1 - y, c), (CORE,), z - k + 1 >= 0)
            pass_on(tile(z + k - 1, 1 - y, c), (CORE,), z + k - 1 < depth)
        if k == 2:
            for step in range(1, tiles):
                gram_copy(peer_of(step)[0], step).wait_recv()
            corner_moves(grams, moved, wide, nodes, width)
            assemble(moved, stiff, nodes, width, pairs[:4])
    assemble(moved, stiff, nodes, width, pairs[4:])
    k = depth
    pass_on(tile(z - k + 1, 1 - y, c), (CORE,), z - k + 1 >= 0)
    pass_on(tile(z + k - 1, 1 - y, c), (CORE,), z + k - 1 < depth)
    for zz in range(depth):
        for yy in range(2):
            pass_on(tile(zz, yy, 1 - c), ())

    @pl.when(is_owner)
    def _():
        picked[...] = held[:, :, pl.ds(first_column, 128)]

    @pl.when(jnp.logical_not(is_owner))
    def _():
        for t in range(tiles):
            block_copy(t, PEER).wait_recv()

    chosen = picked[...].reshape(3 * nodes, 128)
    turned = lax.dot_general(
        chosen, stiff[...], (((0,), (0,)), ((), ())), preferred_element_type=jnp.float32
    )
    wide[0:128, :] = turned.astype(jnp.bfloat16)
    product = jnp.dot(
        wide[...], held[...].reshape(3 * nodes, share), preferred_element_type=jnp.float32
    )
    hess_ref[...] = product[:128].T
    line[...] = jnp.broadcast_to(product[128:129] + product[129:130], (8, share))
    pair = line[0:1, pl.ds(pl.multiple_of((mine // 2) * 128, 128), 128)]
    pair = jnp.where(mine % 2 == 1, pltpu.roll(pair, 64, 1), pair)
    grad_ref[...] = pair[:, :64]

    for when, copy, t, way in sent:
        guarded(when, lambda: copy(t, way).wait_send())
    for step in range(1, tiles):
        gram_copy(mine, step).wait_send()


def hand_over(hess_ref, grad_ref, hess_out, grad_out, hess, grad, in_sem, out_sem):
    pieces = 8
    height = hess.shape[0] // pieces
    steps = [(hess_ref.at[pl.ds(i * height, height)], hess.at[pl.ds(i * height, height)],
              hess_out.at[pl.ds(i * height, height)]) for i in range(pieces)]
    steps.append((grad_ref, grad, grad_out))
    arriving = [pltpu.make_async_copy(s[0], s[1], in_sem.at[i]) for i, s in enumerate(steps)]
    leaving = [pltpu.make_async_copy(s[1], s[2], out_sem.at[i]) for i, s in enumerate(steps)]
    for copy in arriving:
        copy.start()
    for one, other in zip(arriving, leaving):
        one.wait()
        other.start()
    for copy in leaving:
        copy.wait()


def gathered(sizes, coefficients, noise_sigma, residual, crack_mask, node_panel):
    depth, columns, share = sizes
    tiles = depth * columns
    nodes = tiles * 16
    panel = node_panel[0].transpose(1, 0, 2)
    hessian, gradient = pl.pallas_call(
        functools.partial(kernel, sizes),
        out_shape=(
            jax.ShapeDtypeStruct((share, 128), jnp.float32),
            jax.ShapeDtypeStruct((1, 64), jnp.float32),
        ),
        in_specs=[pl.BlockSpec(memory_space=pltpu.HBM)] * 5,
        out_specs=[pl.BlockSpec(memory_space=pltpu.VMEM)] * 2,
        scratch_shapes=[
            pltpu.VMEM(coefficients.shape, jnp.bfloat16),
            pltpu.VMEM(noise_sigma.shape, jnp.float32),
            pltpu.VMEM(residual.shape, jnp.float32),
            pltpu.VMEM((1, EL), jnp.int32),
            pltpu.VMEM((3, nodes, share), jnp.bfloat16),
            pltpu.VMEM((3, nodes, 128), jnp.bfloat16),
            pltpu.VMEM((nodes, 128), jnp.float32),
            pltpu.VMEM((4, 128, nodes), jnp.float32),
            pltpu.VMEM((3 * nodes, 3 * nodes), jnp.bfloat16),
            pltpu.VMEM((144, 3 * nodes), jnp.bfloat16),
            pltpu.VMEM((8, share), jnp.float32),
            pltpu.SemaphoreType.DMA((5,)),
            pltpu.SemaphoreType.DMA((5, tiles)),
            pltpu.SemaphoreType.DMA((tiles,)),
            pltpu.SemaphoreType.DMA((tiles,)),
            pltpu.SemaphoreType.DMA((tiles,)),
            pltpu.SemaphoreType.DMA((tiles,)),
        ],
        compiler_params=pltpu.CompilerParams(
            collective_id=0, has_side_effects=True, vmem_limit_bytes=60 * 2**20
        ),
    )(coefficients, noise_sigma, residual, crack_mask.reshape(1, EL), panel)
    hessian, gradient = pl.pallas_call(
        hand_over,
        out_shape=(
            jax.ShapeDtypeStruct((share, 128), jnp.float32),
            jax.ShapeDtypeStruct((1, 64), jnp.float32),
        ),
        in_specs=[pl.BlockSpec(memory_space=pltpu.HBM)] * 2,
        out_specs=[pl.BlockSpec(memory_space=pltpu.HBM)] * 2,
        scratch_shapes=[
            pltpu.VMEM((share, 128), jnp.float32),
            pltpu.VMEM((1, 64), jnp.float32),
            pltpu.SemaphoreType.DMA((9,)),
            pltpu.SemaphoreType.DMA((9,)),
        ],
        compiler_params=pltpu.CompilerParams(vmem_limit_bytes=60 * 2**20),
    )(hessian, gradient)
    return hessian, gradient.reshape(64)


def solution(mesh):
    def on_device(coefficients, noise_sigma, residual, crack_mask, node_panel):
        depth, columns, share = mesh.shape["row"], mesh.shape["col"], node_panel.shape[3]
        fits = (
            mesh.shape["param"] == 2
            and columns == 4
            and depth >= 3
            and noise_sigma.shape == (CAMS, EL, 128)
            and node_panel.shape[:3] == (1, 16, 3)
            and share == 64 * depth * columns
        )
        if fits:
            return gathered(
                (depth, columns, share), coefficients, noise_sigma, residual, crack_mask, node_panel
            )
        return plain(coefficients, noise_sigma, residual, crack_mask, node_panel)

    in_specs = (
        P(None, None, "row", "col"),
        P(None, "row", "col"),
        P(None, "row", "col"),
        P("row", "col"),
        P("row", "col", None, "param"),
    )
    out_specs = (P("param", ("row", "col")), P(("param", "row", "col")))
    return jax.shard_map(
        on_device, mesh=mesh, in_specs=in_specs, out_specs=out_specs, check_vma=False
    )
```
